512 devices in a mesh: own: 32 (over y, z_hi), blk: 16 (over x, z_lo, core).
Axes of the slice: x: 4, y: 8, z: 8 (z_hi: 4, z_lo: 2; z = z_hi * 2 + z_lo), core: 2. Of those that a mesh axis runs over, the one named last changes fastest.
Arguments:
- points: bfloat16 [64, 65536], P(None, ('own', 'blk')), may hold values from -6 to 6
- solution_field: float32 [33, 65536], P(None, ('own', 'blk')), may hold values from -6 to 6
- residual: float32 [33, 65536], P(None, ('own', 'blk')), may hold values from -12 to 12
- direction: float32 [33, 65536], P(None, ('own', 'blk')), may hold values from -12 to 12
Outputs:
- solution_next: float32 [33, 65536], P(None, ('own', 'blk'))
- residual_next: float32 [33, 65536], P(None, ('own', 'blk'))
- direction_next: float32 [33, 65536], P(None, ('own', 'blk'))
The draws below stay inside these ranges and needn't reach their ends.
All inputs are finite; a program needn't handle non-finite values.
Results may differ from the reference program's by a relative error of at most 0.0027.
Values may be sent and summed in bfloat16 or wider, within the bound.
No kernel may reach another device: no remote copies, remote signals or barrier semaphores. Data moves between devices by JAX's collectives and lax.ppermute only.
A program may use at most 64 MiB of HBM per device.

```python
import math
import jax
import jax.numpy as jnp
from jax import lax

DIM = 64
RHS = 33
POINTS = 65536


def rising_field(key):
    index = jnp.arange(POINTS, dtype=jnp.float32)
    scale = 1.0 + 2.0 * index / (POINTS - 1)
    base = jax.random.truncated_normal(key, -4.0, 4.0, (RHS, POINTS), jnp.float32)
    return base * scale[None, :]


def draw_residual(key, part):
    return rising_field(jax.random.fold_in(key, 11))


def draw_direction(key, part):
    return rising_field(jax.random.fold_in(key, 23))


def levels(key, shape, shards, smallest, largest):
    loudness = 1.0
    for axis_at, shards_of in shards:
        draws = jax.random.uniform(jax.random.fold_in(jax.random.fold_in(key, 6), axis_at), (shards_of,), jnp.float32, smallest / len(shards), largest / len(shards))
        loudness = loudness * jnp.repeat(jnp.exp(draws), shape[axis_at] // shards_of).reshape((-1,) + (1,) * (len(shape) - 1 - axis_at))
    return loudness


def normal_values(own_key, shape, scale, most, pieces=(), kind=jnp.bfloat16):
    level = levels(own_key, shape, pieces, -0.22, 0.18) if pieces else 1.0
    array = jax.random.normal(own_key, shape, jnp.float32) * scale * level
    return jnp.minimum(jnp.maximum(array, -most), most).astype(kind)


def setup_inputs(seed: int = 0) -> dict:
    key_list = jax.random.split(jax.random.key(seed), 5)
    return {
        "points": normal_values(key_list[0], (DIM, POINTS), 1.0, 6.0, ((1, 512),)),
        "solution_field": normal_values(key_list[1], (RHS, POINTS), 1.0, 6.0, ((1, 512),), jnp.float32),
        "residual": draw_residual(jax.random.fold_in(key_list[4], 71), 0),
        "direction": draw_direction(jax.random.fold_in(key_list[4], 71), 0),
    }


amplitude = 1.0
decay_rate = 1.0 / 16.0
noise_level = 0.5


def tile_products(row_blocks, row_norms, columns, dirs):
    col_norms = jnp.sum(jnp.square(columns.astype(jnp.float32)), axis=0)

    def single(pair):
        rows, norms = pair
        inner = lax.dot_general(rows, columns, (((0,), (0,)), ((), ())), preferred_element_type=jnp.float32)
        dist = jnp.maximum(norms[:, None] + col_norms[None, :] - 2.0 * inner, 0.0)
        kern = (amplitude * jnp.exp(-decay_rate * dist)).astype(jnp.bfloat16)
        return lax.dot_general(dirs, kern, (((1,), (1,)), ((), ())), preferred_element_type=jnp.float32)

    return lax.map(single, (row_blocks, row_norms))


def reference(points, solution_field, residual, direction):
    width = points.shape[1]
    size = math.gcd(width, 512)
    count = width // size
    blocks = points.reshape(points.shape[0], count, size).transpose(1, 0, 2)
    norms = jnp.sum(jnp.square(blocks.astype(jnp.float32)), axis=1)
    dir_low = direction.astype(jnp.bfloat16)
    prods = tile_products(blocks, norms, points, dir_low)
    image = prods.transpose(1, 0, 2).reshape(direction.shape[0], width) + noise_level * direction
    rr_sum = jnp.sum(residual * residual, axis=1)
    pq_sum = jnp.sum(direction * image, axis=1)
    alpha = (rr_sum / pq_sum)[:, None]
    solution_next = solution_field + alpha * direction
    residual_next = residual - alpha * image
    new_sum = jnp.sum(residual_next * residual_next, axis=1)
    direction_next = residual_next + (new_sum / rr_sum)[:, None] * direction
    return solution_next, residual_next, direction_next
```

```python
import functools
import math

import jax
import jax.numpy as jnp
from jax import lax
from jax.experimental import pallas as pl
from jax.experimental.pallas import tpu as pltpu
from jax.sharding import Mesh
from jax.sharding import PartitionSpec as P

f32 = jnp.float32
bf16 = jnp.bfloat16

ALL = ("y", "zh", "x", "zl", "c")
COLS = ("y", "zh")
ROWS = ("x", "zl", "c")
SUM_1 = ("y", "x")
SUM_2 = ("zh", "zl", "c")

amplitude = 1.0
decay_rate = 1.0 / 16.0
noise_level = 0.5
LOG2E = math.log2(math.e)
DEPTH = 128
LANES = 128
ROW_BLOCK = 512
COL_BLOCK = 4096
VMEM = 50 * 2**20


def copies(shard, axes):
    peers = lax.axis_size(axes)
    return lax.all_to_all(
        jnp.broadcast_to(shard[None], (peers, *shard.shape)), axes, 0, 0, tiled=True
    )


def norm_features(x, first):
    values = x.astype(f32)
    norms = jnp.sum(values * values, axis=0, keepdims=True) * (-decay_rate)
    high = norms.astype(bf16).astype(f32)
    middle = (norms - high).astype(bf16).astype(f32)
    low = norms - high - middle
    at = lax.broadcasted_iota(jnp.int32, x.shape, 0)
    ones = 3 - first
    out = jnp.where((at >= ones) & (at < ones + 3), 1.0, 0.0)
    for k, piece in enumerate((high, middle, low)):
        out = jnp.where(at == first + k, piece, out)
    return out.astype(bf16)


def product_kernel(rows_ref, cols_ref, out_ref, row_side, col_side, dirs):
    dim = rows_ref.shape[1]
    rhs = dirs.shape[0]

    def one_row_block(k, carry):
        x = rows_ref[k]
        here = pl.ds(pl.multiple_of(k * LANES, LANES), LANES)
        row_side[0:dim, here] = (x.astype(f32) * (2.0 * decay_rate)).astype(bf16)
        row_side[dim:DEPTH, here] = norm_features(x, 0)
        return carry

    def one_col_block(k, carry):
        both = cols_ref[k]
        x = both[0:dim]
        here = pl.ds(pl.multiple_of(k * LANES, LANES), LANES)
        col_side[here, :] = jnp.concatenate([x, norm_features(x, 3)], axis=0).T
        dirs[:, here] = both[dim : dim + rhs]
        return carry

    lax.fori_loop(0, rows_ref.shape[0], one_row_block, 0, unroll=4)
    lax.fori_loop(0, cols_ref.shape[0], one_col_block, 0, unroll=4)
    width = row_side.shape[1]
    depth = col_side.shape[0]

    def one_step(i, carry):
        here = pl.ds(pl.multiple_of(i * ROW_BLOCK, ROW_BLOCK), ROW_BLOCK)
        side = row_side[:, here]
        total = jnp.zeros((rhs, ROW_BLOCK), f32)
        for j in range(depth // COL_BLOCK):
            there = pl.ds(j * COL_BLOCK, COL_BLOCK)
            expo = jnp.dot(col_side[there, :], side, preferred_element_type=f32)
            kern = jnp.minimum((amplitude * jnp.exp2(expo * LOG2E)).astype(bf16), jnp.asarray(amplitude, bf16))
            total = total + jnp.dot(dirs[:, there], kern, preferred_element_type=f32)
        for k in range(ROW_BLOCK // LANES):
            out_ref[i * (ROW_BLOCK // LANES) + k] = total[:, k * LANES : (k + 1) * LANES]
        return carry

    lax.fori_loop(0, width // ROW_BLOCK, one_step, 0)


def partial_products(rows, cols):
    count_r, dim, _ = rows.shape
    count_c = cols.shape[0]
    rhs = cols.shape[1] - dim
    pairs = count_r * count_c * LANES * LANES
    return pl.pallas_call(
        product_kernel,
        out_shape=jax.ShapeDtypeStruct((count_r, rhs, LANES), f32),
        in_specs=[pl.BlockSpec(memory_space=pltpu.VMEM)] * 2,
        out_specs=pl.BlockSpec(memory_space=pltpu.VMEM),
        scratch_shapes=[
            pltpu.VMEM((DEPTH, count_r * LANES), bf16),
            pltpu.VMEM((count_c * LANES, DEPTH), bf16),
            pltpu.VMEM((rhs, count_c * LANES), bf16),
        ],
        compiler_params=pltpu.CompilerParams(vmem_limit_bytes=VMEM),
        cost_estimate=pl.CostEstimate(flops=2 * pairs * (DEPTH + rhs), bytes_accessed=2 * 2**20, transcendentals=pairs),
        name="products",
    )(rows, cols)


def local(points, solution_field, residual, direction):
    rhs = direction.shape[0]
    packed = jnp.concatenate([points, direction.astype(bf16)], axis=0)
    cols = copies(packed, COLS)
    rows = lax.all_gather(points[None], ("zl", "c"), axis=0, tiled=True)
    rows = lax.all_gather(rows, "x", axis=0, tiled=True)
    partial = partial_products(rows, cols)
    arrived = lax.all_to_all(partial, ROWS, 0, 0, tiled=True)
    image = arrived.sum(axis=0) + noise_level * direction
    sums = jnp.stack(
        [
            jnp.sum(residual * residual, axis=1),
            jnp.sum(direction * image, axis=1),
            jnp.sum(residual * image, axis=1),
            jnp.sum(image * image, axis=1),
        ]
    )
    sums = copies(sums, SUM_1).sum(axis=0)
    sums = copies(sums, SUM_2).sum(axis=0)
    rr_sum, pq_sum, rq_sum, qq_sum = sums[0], sums[1], sums[2], sums[3]
    alpha = rr_sum / pq_sum
    residual_next = residual - alpha[:, None] * image
    new_sum = rr_sum - 2.0 * alpha * rq_sum + alpha * alpha * qq_sum
    solution_next = solution_field + alpha[:, None] * direction
    direction_next = residual_next + (new_sum / rr_sum)[:, None] * direction
    return (solution_next, residual_next, direction_next)


def solution(mesh):
    split = Mesh(mesh.devices.reshape(8, 4, 4, 2, 2), ALL)
    spec = P(None, ALL)
    return jax.shard_map(
        local, mesh=split, in_specs=(spec,) * 4, out_specs=(spec,) * 3, check_vma=False
    )
```

```python
import functools
import math

import jax
import jax.numpy as jnp
from jax import lax
from jax.experimental import pallas as pl
from jax.experimental.pallas import tpu as pltpu
from jax.sharding import Mesh
from jax.sharding import PartitionSpec as P

f32 = jnp.float32
bf16 = jnp.bfloat16

ALL = ("yh", "yl", "zh", "x", "zl", "c")
COLS = ("yh", "zh")
ROWS = ("yl", "x", "zl")
SUM_1 = ("yh", "yl", "x")
SUM_2 = ("zh", "zl", "c")

amplitude = 1.0
decay_rate = 1.0 / 16.0
noise_level = 0.5
LOG2E = math.log2(math.e)
DEPTH = 128
LANES = 128
ROW_BLOCK = 512
VMEM = 50 * 2**20
IN_VMEM = pl.BlockSpec(memory_space=pltpu.VMEM)


def kernel_call(body, out_shape, name, flops=10**6, scratch=()):
    outs = jax.tree.leaves(out_shape)
    return pl.pallas_call(
        body,
        out_shape=out_shape,
        out_specs=jax.tree.map(lambda _: IN_VMEM, out_shape),
        scratch_shapes=scratch,
        compiler_params=pltpu.CompilerParams(vmem_limit_bytes=VMEM),
        cost_estimate=pl.CostEstimate(
            flops=flops, bytes_accessed=sum(o.size * o.dtype.itemsize for o in outs), transcendentals=0
        ),
        name=name,
    )


def norm_features(x, first):
    values = x.astype(f32)
    norms = jnp.sum(values * values, axis=0, keepdims=True) * (-decay_rate)
    high = norms.astype(bf16).astype(f32)
    middle = (norms - high).astype(bf16).astype(f32)
    low = norms - high - middle
    at = lax.broadcasted_iota(jnp.int32, x.shape, 0)
    ones = 3 - first
    out = jnp.where((at >= ones) & (at < ones + 3), 1.0, 0.0)
    for k, piece in enumerate((high, middle, low)):
        out = jnp.where(at == first + k, piece, out)
    return out.astype(bf16)


def pack_kernel(points_ref, direction_ref, cols_ref, rows_ref):
    dim = points_ref.shape[0]
    both = jnp.concatenate([points_ref[...], direction_ref[...].astype(bf16)], axis=0)
    for k in range(cols_ref.shape[0]):
        cols_ref[k] = both
    for k in range(rows_ref.shape[0]):
        rows_ref[k] = both[0:dim]


def product_kernel(rows_ref, near_ref, far_ref, out_ref, row_side, col_side, dirs):
    dim = rows_ref.shape[1]
    rhs = dirs.shape[0]
    peers = near_ref.shape[0]

    def one_row_block(k, carry):
        x = rows_ref[k]
        here = pl.ds(pl.multiple_of(k * LANES, LANES), LANES)
        row_side[0:dim, here] = (x.astype(f32) * (2.0 * decay_rate)).astype(bf16)
        row_side[dim:DEPTH, here] = norm_features(x, 0)
        return carry

    def one_col_block(k, carry):
        for half, ref in enumerate((near_ref, far_ref)):
            both = ref[k]
            x = both[0:dim]
            here = pl.ds(pl.multiple_of((half * peers + k) * LANES, LANES), LANES)
            col_side[here, :] = jnp.concatenate([x, norm_features(x, 3)], axis=0).T
            dirs[:, here] = both[dim : dim + rhs]
        return carry

    lax.fori_loop(0, rows_ref.shape[0], one_row_block, 0, unroll=4)
    lax.fori_loop(0, peers, one_col_block, 0, unroll=2)

    def one_step(i, carry):
        here = pl.ds(pl.multiple_of(i * ROW_BLOCK, ROW_BLOCK), ROW_BLOCK)
        expo = jnp.dot(col_side[...], row_side[:, here], preferred_element_type=f32)
        kern = jnp.minimum((amplitude * jnp.exp2(expo * LOG2E)).astype(bf16), jnp.asarray(amplitude, bf16))
        total = jnp.dot(dirs[...], kern, preferred_element_type=f32)
        for k in range(ROW_BLOCK // LANES):
            out_ref[i * (ROW_BLOCK // LANES) + k] = total[:, k * LANES : (k + 1) * LANES]
        return carry

    lax.fori_loop(0, row_side.shape[1] // ROW_BLOCK, one_step, 0)


def to_lanes(values):
    square = jnp.broadcast_to(values, (values.shape[0], LANES))
    at = lax.broadcasted_iota(jnp.int32, square.shape, 0)
    lane = lax.broadcasted_iota(jnp.int32, square.shape, 1)
    return jnp.sum(jnp.where(at == lane, square, 0.0), axis=0, keepdims=True)


def sums_kernel(arrived_ref, direction_ref, residual_ref, image_ref, sums_ref):
    direction = direction_ref[...]
    residual = residual_ref[...]
    image = noise_level * direction
    total = arrived_ref[0]
    for k in range(1, arrived_ref.shape[0]):
        total = total + arrived_ref[k]
    image = total + image
    image_ref[...] = image
    products = (residual * residual, direction * image, residual * image, image * image)
    rows = [to_lanes(jnp.sum(v, axis=1, keepdims=True)) for v in products]
    sums = jnp.concatenate(rows, axis=0)
    for k in range(sums_ref.shape[0]):
        sums_ref[k] = sums


def middle_kernel(arrived_ref, sums_ref):
    sums = jnp.sum(arrived_ref[...], axis=0)
    for k in range(sums_ref.shape[0]):
        sums_ref[k] = sums


def to_rows(row, rhs):
    square = jnp.broadcast_to(row, (rhs, LANES))
    at = lax.broadcasted_iota(jnp.int32, square.shape, 0)
    lane = lax.broadcasted_iota(jnp.int32, square.shape, 1)
    return jnp.sum(jnp.where(at == lane, square, 0.0), axis=1, keepdims=True)


def last_kernel(arrived_ref, image_ref, solution_ref, residual_ref, direction_ref, s_ref, r_ref, d_ref):
    rhs = image_ref.shape[0]
    sums = jnp.sum(arrived_ref[...], axis=0)
    rr_sum, pq_sum, rq_sum, qq_sum = (to_rows(sums[k : k + 1], rhs) for k in range(4))
    alpha = rr_sum / pq_sum
    beta = (rr_sum - 2.0 * alpha * rq_sum + alpha * alpha * qq_sum) / rr_sum
    direction = direction_ref[...]
    residual_next = residual_ref[...] - alpha * image_ref[...]
    s_ref[...] = solution_ref[...] + alpha * direction
    r_ref[...] = residual_next
    d_ref[...] = residual_next + beta * direction


def local(points, solution_field, residual, direction):
    dim, width = points.shape
    rhs = direction.shape[0]
    peers_c, peers_r = lax.axis_size(COLS), lax.axis_size(ROWS)
    shape = jax.ShapeDtypeStruct
    cols, rows = kernel_call(
        pack_kernel,
        (shape((peers_c, dim + rhs, width), bf16), shape((peers_r, dim, width), bf16)),
        "pack",
    )(points, direction)
    cols = lax.all_to_all(cols, COLS, 0, 0, tiled=True)
    rows = lax.all_to_all(rows, ROWS, 0, 0, tiled=True)
    other = lax.ppermute(cols, "c", [(0, 1), (1, 0)])
    depth = 2 * peers_c * width
    pairs = depth * peers_r * width
    partial = kernel_call(
        product_kernel,
        shape((peers_r, rhs, width), f32),
        "products",
        flops=2 * pairs * (DEPTH + rhs),
        scratch=[
            pltpu.VMEM((DEPTH, peers_r * width), bf16),
            pltpu.VMEM((depth, DEPTH), bf16),
            pltpu.VMEM((rhs, depth), bf16),
        ],
    )(rows, cols, other)
    arrived = lax.all_to_all(partial, ROWS, 0, 0, tiled=True)
    image, sums = kernel_call(
        sums_kernel,
        (shape((rhs, width), f32), shape((lax.axis_size(SUM_1), 4, LANES), f32)),
        "sums",
    )(arrived, direction, residual)
    sums = lax.all_to_all(sums, SUM_1, 0, 0, tiled=True)
    sums = kernel_call(middle_kernel, shape((lax.axis_size(SUM_2), 4, LANES), f32), "middle")(sums)
    sums = lax.all_to_all(sums, SUM_2, 0, 0, tiled=True)
    out = shape((rhs, width), f32)
    return kernel_call(last_kernel, (out, out, out), "last")(
        sums, image, solution_field, residual, direction
    )


def solution(mesh):
    split = Mesh(mesh.devices.reshape(4, 2, 4, 4, 2, 2), ALL)
    spec = P(None, ALL)
    return jax.shard_map(
        local, mesh=split, in_specs=(spec,) * 4, out_specs=(spec,) * 3, check_vma=False
    )
```

```python
import functools
import math

import jax
import jax.numpy as jnp
import numpy as np
from jax import lax
from jax.experimental import pallas as pl
from jax.experimental.pallas import tpu as pltpu
from jax.sharding import Mesh
from jax.sharding import PartitionSpec as P

f32 = jnp.float32
bf16 = jnp.bfloat16

ALL = ("yh", "yl", "zh", "x", "zl", "c")
SIZES = (4, 2, 4, 4, 2, 2)
ROWS = ("yl", "x", "zl")
SUM_1 = ("zh", "zl", "c")
SUM_2 = ("yh", "yl", "x")

amplitude = 1.0
decay_rate = 1.0 / 16.0
noise_level = 0.5
LOG2E = math.log2(math.e)
DEPTH = 128
LANES = 128
ROW_BLOCK = 1024
VMEM = 50 * 2**20
IN_VMEM = pl.BlockSpec(memory_space=pltpu.VMEM)


def kernel_call(body, out_shape, name, flops=10**6, scratch=(), in_specs=None):
    outs = jax.tree.leaves(out_shape)
    specs = {} if in_specs is None else {"in_specs": in_specs}
    return pl.pallas_call(
        body,
        out_shape=out_shape,
        **specs,
        out_specs=jax.tree.map(lambda _: IN_VMEM, out_shape),
        scratch_shapes=scratch,
        compiler_params=pltpu.CompilerParams(vmem_limit_bytes=VMEM),
        cost_estimate=pl.CostEstimate(
            flops=flops, bytes_accessed=sum(o.size * o.dtype.itemsize for o in outs), transcendentals=0
        ),
        name=name,
    )


def norm_features(x, first):
    values = x.astype(f32)
    norms = jnp.sum(values * values, axis=0, keepdims=True) * (-decay_rate)
    high = norms.astype(bf16).astype(f32)
    middle = (norms - high).astype(bf16).astype(f32)
    low = norms - high - middle
    at = lax.broadcasted_iota(jnp.int32, x.shape, 0)
    ones = 3 - first
    out = jnp.where((at >= ones) & (at < ones + 3), 1.0, 0.0)
    for k, piece in enumerate((high, middle, low)):
        out = jnp.where(at == first + k, piece, out)
    return out.astype(bf16)


def far_and_near():
    at = np.arange(math.prod(SIZES)).reshape(SIZES)
    far = at[..., 0].transpose(1, 3, 4, 0, 2).reshape(-1, SIZES[0] * SIZES[2])
    near = at[..., 1].transpose(0, 2, 1, 3, 4).reshape(far.shape)
    return np.concatenate([far, near]).tolist()


def product_kernel(core_ref, mine_ref, other_ref, out_ref, row_side, col_side, dirs):
    core = core_ref[0]
    rhs = dirs.shape[0]
    dim = DEPTH // 2
    peers = mine_ref.shape[0] // 2

    def prepare(rows_ref, cols_ref, at):
        def one_block(k, carry):
            x = rows_ref[2 * k + at][0:dim]
            here = pl.ds(pl.multiple_of(k * LANES, LANES), LANES)
            row_side[0:dim, here] = (x.astype(f32) * (2.0 * decay_rate)).astype(bf16)
            row_side[dim:DEPTH, here] = norm_features(x, 0)
            for half in range(2):
                both = cols_ref[2 * k + half]
                x = both[0:dim]
                here = pl.ds(pl.multiple_of((half * peers + k) * LANES, LANES), LANES)
                col_side[here, :] = jnp.concatenate([x, norm_features(x, 3)], axis=0).T
                dirs[:, here] = both[dim : dim + rhs]
            return carry

        lax.fori_loop(0, peers, one_block, 0, unroll=2)

    @pl.when(core == 0)
    def _():
        prepare(other_ref, mine_ref, 0)

    @pl.when(core == 1)
    def _():
        prepare(mine_ref, other_ref, 1)

    def one_step(i, carry):
        here = pl.ds(pl.multiple_of(i * ROW_BLOCK, ROW_BLOCK), ROW_BLOCK)
        expo = jnp.dot(col_side[...], row_side[:, here], preferred_element_type=f32)
        kern = jnp.minimum((amplitude * jnp.exp2(expo * LOG2E)).astype(bf16), jnp.asarray(amplitude, bf16))
        total = jnp.dot(dirs[...], kern, preferred_element_type=f32)
        for k in range(ROW_BLOCK // LANES):
            out_ref[i * (ROW_BLOCK // LANES) + k] = total[:, k * LANES : (k + 1) * LANES]
        return carry

    lax.fori_loop(0, row_side.shape[1] // ROW_BLOCK, one_step, 0)


def to_lanes(values):
    square = jnp.broadcast_to(values, (values.shape[0], LANES))
    at = lax.broadcasted_iota(jnp.int32, square.shape, 0)
    lane = lax.broadcasted_iota(jnp.int32, square.shape, 1)
    return jnp.sum(jnp.where(at == lane, square, 0.0), axis=0, keepdims=True)


def sums_kernel(arrived_ref, direction_ref, residual_ref, image_ref, sums_ref):
    direction = direction_ref[...]
    residual = residual_ref[...]
    image = noise_level * direction
    total = arrived_ref[0]
    for k in range(1, arrived_ref.shape[0]):
        total = total + arrived_ref[k]
    image = total + image
    image_ref[...] = image
    products = (residual * residual, direction * image, residual * image, image * image)
    rows = [to_lanes(jnp.sum(v, axis=1, keepdims=True)) for v in products]
    sums = jnp.concatenate(rows, axis=0)
    for k in range(sums_ref.shape[0]):
        sums_ref[k] = sums


def middle_kernel(arrived_ref, sums_ref):
    sums = jnp.sum(arrived_ref[...], axis=0)
    for k in range(sums_ref.shape[0]):
        sums_ref[k] = sums


def to_rows(row, rhs):
    square = jnp.broadcast_to(row, (rhs, LANES))
    at = lax.broadcasted_iota(jnp.int32, square.shape, 0)
    lane = lax.broadcasted_iota(jnp.int32, square.shape, 1)
    return jnp.sum(jnp.where(at == lane, square, 0.0), axis=1, keepdims=True)


def last_kernel(arrived_ref, image_ref, solution_ref, residual_ref, direction_ref, s_ref, r_ref, d_ref):
    rhs = image_ref.shape[0]
    sums = jnp.sum(arrived_ref[...], axis=0)
    rr_sum, pq_sum, rq_sum, qq_sum = (to_rows(sums[k : k + 1], rhs) for k in range(4))
    alpha = rr_sum / pq_sum
    beta = (rr_sum - 2.0 * alpha * rq_sum + alpha * alpha * qq_sum) / rr_sum
    direction = direction_ref[...]
    residual_next = residual_ref[...] - alpha * image_ref[...]
    s_ref[...] = solution_ref[...] + alpha * direction
    r_ref[...] = residual_next
    d_ref[...] = residual_next + beta * direction


def local(points, solution_field, residual, direction):
    dim, width = points.shape
    rhs = direction.shape[0]
    shape = jax.ShapeDtypeStruct
    both = jnp.concatenate([points, direction.astype(bf16)], axis=0)
    groups = far_and_near()
    peers = len(groups[0])
    both = lax.all_gather(jnp.pad(both, ((0, -both.shape[0] % 8), (0, 0))), "c", axis=0, tiled=True)
    both = both.reshape(2, -1, both.shape[1])
    mine = jnp.broadcast_to(both[None], (peers, *both.shape)).reshape(-1, *both.shape[1:])
    mine = lax.all_to_all(mine, ALL, 0, 0, axis_index_groups=groups, tiled=True)
    other = lax.ppermute(mine, "c", [(0, 1), (1, 0)])
    depth = 2 * peers * width
    pairs = depth * peers * width
    partial = kernel_call(
        product_kernel,
        shape((peers, rhs, width), f32),
        "products",
        flops=2 * pairs * (DEPTH + rhs),
        scratch=[
            pltpu.VMEM((DEPTH, peers * width), bf16),
            pltpu.VMEM((depth, DEPTH), bf16),
            pltpu.VMEM((rhs, depth), bf16),
        ],
        in_specs=[pl.BlockSpec(memory_space=pltpu.SMEM), IN_VMEM, IN_VMEM],
    )(lax.axis_index("c").reshape(1), mine, other)
    arrived = lax.all_to_all(partial, ROWS, 0, 0, tiled=True)
    image, sums = kernel_call(
        sums_kernel,
        (shape((rhs, width), f32), shape((lax.axis_size(SUM_1), 4, LANES), f32)),
        "sums",
    )(arrived, direction, residual)
    sums = lax.all_to_all(sums, SUM_1, 0, 0, tiled=True)
    sums = kernel_call(middle_kernel, shape((lax.axis_size(SUM_2), 4, LANES), f32), "middle")(sums)
    sums = lax.all_to_all(sums, SUM_2, 0, 0, tiled=True)
    out = shape((rhs, width), f32)
    return kernel_call(last_kernel, (out, out, out), "last")(
        sums, image, solution_field, residual, direction
    )


def solution(mesh):
    split = Mesh(mesh.devices.reshape(SIZES), ALL)
    spec = P(None, ALL)
    return jax.shard_map(
        local, mesh=split, in_specs=(spec,) * 4, out_specs=(spec,) * 3, check_vma=False
    )
```

```python
import functools
import math

import jax
import jax.numpy as jnp
import numpy as np
from jax import lax
from jax.experimental import pallas as pl
from jax.experimental.pallas import tpu as pltpu
from jax.sharding import Mesh
from jax.sharding import PartitionSpec as P

f32 = jnp.float32
bf16 = jnp.bfloat16

ALL = ("yh", "yl", "zh", "x", "zl", "c")
SIZES = (4, 2, 4, 4, 2, 2)
ROWS = ("yl", "x", "zl")
SUM_1 = ("zh", "zl", "c")
SUM_2 = ("yh", "yl", "x")

amplitude = 1.0
decay_rate = 1.0 / 16.0
noise_level = 0.5
LOG2E = math.log2(math.e)
DEPTH = 128
LANES = 128
ROW_BLOCK = 1024
COL_CHUNKS = 4
VMEM = 50 * 2**20
IN_VMEM = pl.BlockSpec(memory_space=pltpu.VMEM)


def kernel_call(body, out_shape, name, flops=10**6, scratch=(), in_specs=None):
    outs = jax.tree.leaves(out_shape)
    specs = {} if in_specs is None else {"in_specs": in_specs}
    return pl.pallas_call(
        body,
        out_shape=out_shape,
        **specs,
        out_specs=jax.tree.map(lambda _: IN_VMEM, out_shape),
        scratch_shapes=scratch,
        compiler_params=pltpu.CompilerParams(vmem_limit_bytes=VMEM),
        cost_estimate=pl.CostEstimate(
            flops=flops, bytes_accessed=sum(o.size * o.dtype.itemsize for o in outs), transcendentals=0
        ),
        name=name,
    )


def norm_features(x, first):
    values = x.astype(f32)
    norms = jnp.sum(values * values, axis=0, keepdims=True) * (-decay_rate)
    high = norms.astype(bf16).astype(f32)
    middle = (norms - high).astype(bf16).astype(f32)
    low = norms - high - middle
    at = lax.broadcasted_iota(jnp.int32, x.shape, 0)
    ones = 3 - first
    out = jnp.where((at >= ones) & (at < ones + 3), 1.0, 0.0)
    for k, piece in enumerate((high, middle, low)):
        out = jnp.where(at == first + k, piece, out)
    return out.astype(bf16)


def far_and_near():
    at = np.arange(math.prod(SIZES)).reshape(SIZES)
    far = at[..., 0].transpose(1, 3, 4, 0, 2).reshape(-1, SIZES[0] * SIZES[2])
    near = at[..., 1].transpose(0, 2, 1, 3, 4).reshape(far.shape)
    return np.concatenate([far, near]).tolist()


def product_kernel(core_ref, mine_ref, other_ref, out_ref, row_side, col_side, dirs):
    first = core_ref[0] == 0
    rhs = dirs.shape[0]
    dim = DEPTH // 2
    count_r = row_side.shape[1] // LANES
    count_c = col_side.shape[0] // LANES
    per_step = ROW_BLOCK // LANES

    def prepare_rows(k):
        x = jnp.where(first, other_ref[2 * k][0:dim], mine_ref[2 * k + 1][0:dim])
        here = slice(k * LANES, (k + 1) * LANES)
        row_side[0:dim, here] = (x.astype(f32) * (2.0 * decay_rate)).astype(bf16)
        row_side[dim:DEPTH, here] = norm_features(x, 0)

    def prepare_cols(k):
        both = jnp.where(first, mine_ref[k], other_ref[k])
        x = both[0:dim]
        here = slice(k * LANES, (k + 1) * LANES)
        col_side[here, :] = jnp.concatenate([x, norm_features(x, 3)], axis=0).T
        dirs[:, here] = both[dim : dim + rhs]

    def products(rows, cols):
        expo = jnp.dot(col_side[cols, :], row_side[:, rows], preferred_element_type=f32)
        kern = jnp.minimum((amplitude * jnp.exp2(expo * LOG2E)).astype(bf16), jnp.asarray(amplitude, bf16))
        return jnp.dot(dirs[:, cols], kern, preferred_element_type=f32)

    def store(i, total):
        for k in range(per_step):
            out_ref[i * per_step + k] = total[:, k * LANES : (k + 1) * LANES]

    chunk = count_c // COL_CHUNKS
    later = list(range(per_step, count_r))
    share = -(-len(later) // COL_CHUNKS)
    for k in range(per_step):
        prepare_rows(k)
    for k in range(chunk):
        prepare_cols(k)
    total = jnp.zeros((rhs, ROW_BLOCK), f32)
    for q in range(COL_CHUNKS):
        if q + 1 < COL_CHUNKS:
            for k in range((q + 1) * chunk, (q + 2) * chunk):
                prepare_cols(k)
        for k in later[q * share : (q + 1) * share]:
            prepare_rows(k)
        cols = slice(q * chunk * LANES, (q + 1) * chunk * LANES)
        total = total + products(slice(0, ROW_BLOCK), cols)
    store(0, total)

    def one_step(i, carry):
        here = pl.ds(pl.multiple_of(i * ROW_BLOCK, ROW_BLOCK), ROW_BLOCK)
        store(i, products(here, slice(0, count_c * LANES)))
        return carry

    lax.fori_loop(1, count_r // per_step, one_step, 0)


def to_lanes(first, second):
    shape = (first.shape[0], LANES)
    at = lax.broadcasted_iota(jnp.int32, shape, 0)
    lane = lax.broadcasted_iota(jnp.int32, shape, 1)
    square = jnp.where(at == lane, first, jnp.where(at + LANES // 2 == lane, second, 0.0))
    return jnp.sum(square, axis=0, keepdims=True)


def sums_kernel(arrived_ref, direction_ref, residual_ref, image_ref, sums_ref):
    direction = direction_ref[...]
    residual = residual_ref[...]
    image = noise_level * direction
    total = arrived_ref[0]
    for k in range(1, arrived_ref.shape[0]):
        total = total + arrived_ref[k]
    image = total + image
    image_ref[...] = image
    products = (residual * residual, direction * image, residual * image, image * image)
    rr_sum, pq_sum, rq_sum, qq_sum = (jnp.sum(v, axis=1, keepdims=True) for v in products)
    sums = jnp.concatenate([to_lanes(rr_sum, pq_sum), to_lanes(rq_sum, qq_sum)], axis=0)
    for k in range(sums_ref.shape[0]):
        sums_ref[k] = sums


def middle_kernel(arrived_ref, sums_ref):
    sums = jnp.sum(arrived_ref[...], axis=0)
    for k in range(sums_ref.shape[0]):
        sums_ref[k] = sums


def to_rows(row, rhs):
    square = jnp.broadcast_to(row, (rhs, LANES))
    at = lax.broadcasted_iota(jnp.int32, square.shape, 0)
    lane = lax.broadcasted_iota(jnp.int32, square.shape, 1)
    return (
        jnp.sum(jnp.where(at == lane, square, 0.0), axis=1, keepdims=True),
        jnp.sum(jnp.where(at + LANES // 2 == lane, square, 0.0), axis=1, keepdims=True),
    )


def last_kernel(arrived_ref, image_ref, solution_ref, residual_ref, direction_ref, s_ref, r_ref, d_ref):
    rhs = image_ref.shape[0]
    sums = jnp.sum(arrived_ref[...], axis=0)
    rr_sum, pq_sum = to_rows(sums[0:1], rhs)
    rq_sum, qq_sum = to_rows(sums[1:2], rhs)
    alpha = rr_sum / pq_sum
    beta = (rr_sum - 2.0 * alpha * rq_sum + alpha * alpha * qq_sum) / rr_sum
    direction = direction_ref[...]
    residual_next = residual_ref[...] - alpha * image_ref[...]
    s_ref[...] = solution_ref[...] + alpha * direction
    r_ref[...] = residual_next
    d_ref[...] = residual_next + beta * direction


def local(points, solution_field, residual, direction):
    dim, width = points.shape
    rhs = direction.shape[0]
    shape = jax.ShapeDtypeStruct
    both = jnp.concatenate([points, direction.astype(bf16)], axis=0)
    groups = far_and_near()
    peers = len(groups[0])
    both = lax.all_gather(jnp.pad(both, ((0, -both.shape[0] % 8), (0, 0))), "c", axis=0, tiled=True)
    both = both.reshape(2, -1, both.shape[1])
    mine = jnp.broadcast_to(both[None], (peers, *both.shape)).reshape(-1, *both.shape[1:])
    mine = lax.all_to_all(mine, ALL, 0, 0, axis_index_groups=groups, tiled=True)
    other = lax.ppermute(mine, "c", [(0, 1), (1, 0)])
    depth = 2 * peers * width
    pairs = depth * peers * width
    partial = kernel_call(
        product_kernel,
        shape((peers, rhs, width), f32),
        "products",
        flops=2 * pairs * (DEPTH + rhs),
        scratch=[
            pltpu.VMEM((DEPTH, peers * width), bf16),
            pltpu.VMEM((depth, DEPTH), bf16),
            pltpu.VMEM((rhs, depth), bf16),
        ],
        in_specs=[pl.BlockSpec(memory_space=pltpu.SMEM), IN_VMEM, IN_VMEM],
    )(lax.axis_index("c").reshape(1), mine, other)
    arrived = lax.all_to_all(partial, ROWS, 0, 0, tiled=True)
    image, sums = kernel_call(
        sums_kernel,
        (shape((rhs, width), f32), shape((lax.axis_size(SUM_1), 2, LANES), f32)),
        "sums",
    )(arrived, direction, residual)
    sums = lax.all_to_all(sums, SUM_1, 0, 0, tiled=True)
    sums = kernel_call(middle_kernel, shape((lax.axis_size(SUM_2), 2, LANES), f32), "middle")(sums)
    sums = lax.all_to_all(sums, SUM_2, 0, 0, tiled=True)
    out = shape((rhs, width), f32)
    return kernel_call(last_kernel, (out, out, out), "last")(
        sums, image, solution_field, residual, direction
    )


def solution(mesh):
    split = Mesh(mesh.devices.reshape(SIZES), ALL)
    spec = P(None, ALL)
    return jax.shard_map(
        local, mesh=split, in_specs=(spec,) * 4, out_specs=(spec,) * 3, check_vma=False
    )
```

```python
import functools
import math

import jax
import jax.numpy as jnp
import numpy as np
from jax import lax
from jax.experimental import pallas as pl
from jax.experimental.pallas import tpu as pltpu
from jax.sharding import Mesh
from jax.sharding import PartitionSpec as P

f32 = jnp.float32
bf16 = jnp.bfloat16

ALL = ("yh", "yl", "zh", "x", "zl", "c")
SIZES = (4, 2, 4, 4, 2, 2)
ROWS = ("yl", "x", "zl")
SUM_1 = ("zh", "zl", "c")
SUM_2 = ("yh", "yl", "x")

amplitude = 1.0
decay_rate = 1.0 / 16.0
noise_level = 0.5
LOG2E = math.log2(math.e)
DEPTH = 128
LANES = 128
ROW_BLOCK = 1024
COL_CHUNKS = 4
VMEM = 50 * 2**20
IN_VMEM = pl.BlockSpec(memory_space=pltpu.VMEM)


def kernel_call(body, out_shape, name, flops=10**6, scratch=(), in_specs=None):
    outs = jax.tree.leaves(out_shape)
    specs = {} if in_specs is None else {"in_specs": in_specs}
    return pl.pallas_call(
        body,
        out_shape=out_shape,
        **specs,
        out_specs=jax.tree.map(lambda _: IN_VMEM, out_shape),
        scratch_shapes=scratch,
        compiler_params=pltpu.CompilerParams(vmem_limit_bytes=VMEM),
        cost_estimate=pl.CostEstimate(
            flops=flops, bytes_accessed=sum(o.size * o.dtype.itemsize for o in outs), transcendentals=0
        ),
        name=name,
    )


def norm_features(x, first):
    values = x.astype(f32)
    norms = jnp.sum(values * values, axis=0, keepdims=True) * (-decay_rate)
    high = norms.astype(bf16).astype(f32)
    middle = (norms - high).astype(bf16).astype(f32)
    low = norms - high - middle
    at = lax.broadcasted_iota(jnp.int32, x.shape, 0)
    ones = 3 - first
    out = jnp.where((at >= ones) & (at < ones + 3), 1.0, 0.0)
    for k, piece in enumerate((high, middle, low)):
        out = jnp.where(at == first + k, piece, out)
    return out.astype(bf16)


def far_and_near():
    at = np.arange(math.prod(SIZES)).reshape(SIZES)
    far = at[..., 0].transpose(1, 3, 4, 0, 2).reshape(-1, SIZES[0] * SIZES[2])
    near = at[..., 1].transpose(0, 2, 1, 3, 4).reshape(far.shape)
    return np.concatenate([far, near]).tolist()


def product_kernel(place_ref, mine_ref, other_ref, out_ref, own_ref, row_side, col_side, dirs, parts):
    first = lax.rem(place_ref[0], 2) == 0
    me = lax.div(place_ref[0], 2)
    rhs = dirs.shape[0]
    dim = DEPTH // 2
    count_r = row_side.shape[1] // LANES
    count_c = col_side.shape[0] // LANES
    per_step = ROW_BLOCK // LANES

    def prepare_rows(k):
        x = jnp.where(first, other_ref[2 * k][0:dim], mine_ref[2 * k + 1][0:dim])
        here = slice(k * LANES, (k + 1) * LANES)
        row_side[0:dim, here] = (x.astype(f32) * (2.0 * decay_rate)).astype(bf16)
        row_side[dim:DEPTH, here] = norm_features(x, 0)

    def prepare_cols(k):
        both = jnp.where(first, mine_ref[k], other_ref[k])
        x = both[0:dim]
        here = slice(k * LANES, (k + 1) * LANES)
        col_side[here, :] = jnp.concatenate([x, norm_features(x, 3)], axis=0).T
        dirs[:, here] = both[dim : dim + rhs]

    def products(rows, cols):
        expo = jnp.dot(col_side[cols, :], row_side[:, rows], preferred_element_type=f32)
        kern = jnp.minimum((amplitude * jnp.exp2(expo * LOG2E)).astype(bf16), jnp.asarray(amplitude, bf16))
        return jnp.dot(dirs[:, cols], kern, preferred_element_type=f32)

    def store(i, total):
        for k in range(per_step):
            part = total[:, k * LANES : (k + 1) * LANES]
            out_ref[i * per_step + k] = part.astype(bf16)
            parts[i * per_step + k] = part

    chunk = count_c // COL_CHUNKS
    later = list(range(per_step, count_r))
    share = -(-len(later) // COL_CHUNKS)
    for k in range(per_step):
        prepare_rows(k)
    for k in range(chunk):
        prepare_cols(k)
    total = jnp.zeros((rhs, ROW_BLOCK), f32)
    for q in range(COL_CHUNKS):
        if q + 1 < COL_CHUNKS:
            for k in range((q + 1) * chunk, (q + 2) * chunk):
                prepare_cols(k)
        for k in later[q * share : (q + 1) * share]:
            prepare_rows(k)
        cols = slice(q * chunk * LANES, (q + 1) * chunk * LANES)
        total = total + products(slice(0, ROW_BLOCK), cols)
    store(0, total)

    def one_step(i, carry):
        here = pl.ds(pl.multiple_of(i * ROW_BLOCK, ROW_BLOCK), ROW_BLOCK)
        store(i, products(here, slice(0, count_c * LANES)))
        return carry

    lax.fori_loop(1, count_r // per_step, one_step, 0)
    own_ref[...] = parts[me]
    out_ref[me] = jnp.zeros((rhs, LANES), bf16)


def to_lanes(first, second):
    shape = (first.shape[0], LANES)
    at = lax.broadcasted_iota(jnp.int32, shape, 0)
    lane = lax.broadcasted_iota(jnp.int32, shape, 1)
    square = jnp.where(at == lane, first, jnp.where(at + LANES // 2 == lane, second, 0.0))
    return jnp.sum(square, axis=0, keepdims=True)


def sums_kernel(arrived_ref, own_ref, direction_ref, residual_ref, image_ref, sums_ref):
    direction = direction_ref[...]
    residual = residual_ref[...]
    image = noise_level * direction
    total = own_ref[...]
    for k in range(arrived_ref.shape[0]):
        total = total + arrived_ref[k].astype(f32)
    image = total + image
    image_ref[...] = image
    products = (residual * residual, direction * image, residual * image, image * image)
    rr_sum, pq_sum, rq_sum, qq_sum = (jnp.sum(v, axis=1, keepdims=True) for v in products)
    sums = jnp.concatenate([to_lanes(rr_sum, pq_sum), to_lanes(rq_sum, qq_sum)], axis=0)
    for k in range(sums_ref.shape[0]):
        sums_ref[k] = sums


def middle_kernel(arrived_ref, sums_ref):
    sums = jnp.sum(arrived_ref[...], axis=0)
    for k in range(sums_ref.shape[0]):
        sums_ref[k] = sums


def to_rows(row, rhs):
    square = jnp.broadcast_to(row, (rhs, LANES))
    at = lax.broadcasted_iota(jnp.int32, square.shape, 0)
    lane = lax.broadcasted_iota(jnp.int32, square.shape, 1)
    return (
        jnp.sum(jnp.where(at == lane, square, 0.0), axis=1, keepdims=True),
        jnp.sum(jnp.where(at + LANES // 2 == lane, square, 0.0), axis=1, keepdims=True),
    )


def last_kernel(arrived_ref, image_ref, solution_ref, residual_ref, direction_ref, s_ref, r_ref, d_ref):
    rhs = image_ref.shape[0]
    sums = jnp.sum(arrived_ref[...], axis=0)
    rr_sum, pq_sum = to_rows(sums[0:1], rhs)
    rq_sum, qq_sum = to_rows(sums[1:2], rhs)
    alpha = rr_sum / pq_sum
    beta = (rr_sum - 2.0 * alpha * rq_sum + alpha * alpha * qq_sum) / rr_sum
    direction = direction_ref[...]
    residual_next = residual_ref[...] - alpha * image_ref[...]
    s_ref[...] = solution_ref[...] + alpha * direction
    r_ref[...] = residual_next
    d_ref[...] = residual_next + beta * direction


def local(points, solution_field, residual, direction):
    dim, width = points.shape
    rhs = direction.shape[0]
    shape = jax.ShapeDtypeStruct
    both = jnp.concatenate([points, direction.astype(bf16)], axis=0)
    groups = far_and_near()
    peers = len(groups[0])
    both = lax.all_gather(jnp.pad(both, ((0, -both.shape[0] % 8), (0, 0))), "c", axis=0, tiled=True)
    both = both.reshape(2, -1, both.shape[1])
    mine = jnp.broadcast_to(both[None], (peers, *both.shape)).reshape(-1, *both.shape[1:])
    mine = lax.all_to_all(mine, ALL, 0, 0, axis_index_groups=groups, tiled=True)
    other = lax.ppermute(mine, "c", [(0, 1), (1, 0)])
    depth = 2 * peers * width
    pairs = depth * peers * width
    place = (2 * lax.axis_index(ROWS) + lax.axis_index("c")).reshape(1)
    partial, own = kernel_call(
        product_kernel,
        (shape((peers, rhs, width), bf16), shape((rhs, width), f32)),
        "products",
        flops=2 * pairs * (DEPTH + rhs),
        scratch=[
            pltpu.VMEM((DEPTH, peers * width), bf16),
            pltpu.VMEM((depth, DEPTH), bf16),
            pltpu.VMEM((rhs, depth), bf16),
            pltpu.VMEM((peers, rhs, width), f32),
        ],
        in_specs=[pl.BlockSpec(memory_space=pltpu.SMEM), IN_VMEM, IN_VMEM],
    )(place, mine, other)
    arrived = lax.all_to_all(partial, ROWS, 0, 0, tiled=True)
    image, sums = kernel_call(
        sums_kernel,
        (shape((rhs, width), f32), shape((lax.axis_size(SUM_1), 2, LANES), f32)),
        "sums",
    )(arrived, own, direction, residual)
    sums = lax.all_to_all(sums, SUM_1, 0, 0, tiled=True)
    sums = kernel_call(middle_kernel, shape((lax.axis_size(SUM_2), 2, LANES), f32), "middle")(sums)
    sums = lax.all_to_all(sums, SUM_2, 0, 0, tiled=True)
    out = shape((rhs, width), f32)
    return kernel_call(last_kernel, (out, out, out), "last")(
        sums, image, solution_field, residual, direction
    )


def solution(mesh):
    split = Mesh(mesh.devices.reshape(SIZES), ALL)
    spec = P(None, ALL)
    return jax.shard_map(
        local, mesh=split, in_specs=(spec,) * 4, out_specs=(spec,) * 3, check_vma=False
    )
```

```python
import functools
import math

import jax
import jax.numpy as jnp
import numpy as np
from jax import lax
from jax.experimental import pallas as pl
from jax.experimental.pallas import tpu as pltpu
from jax.sharding import Mesh
from jax.sharding import PartitionSpec as P

f32 = jnp.float32
bf16 = jnp.bfloat16

ALL = ("y", "zh", "xh", "xl", "zl", "c")
SIZES = (8, 4, 2, 2, 2, 2)
ROWS = ('y', 'xl')
SUM_1 = ("zh", "zl", "c")
SUM_2 = ("y", "xh", "xl")

amplitude = 1.0
decay_rate = 1.0 / 16.0
noise_level = 0.5
LOG2E = math.log2(math.e)
DEPTH = 128
LANES = 128
ROW_BLOCK = 1024
COL_CHUNKS = 4
VMEM = 50 * 2**20
IN_VMEM = pl.BlockSpec(memory_space=pltpu.VMEM)


def kernel_call(body, out_shape, name, flops=10**6, scratch=(), in_specs=None):
    outs = jax.tree.leaves(out_shape)
    specs = {} if in_specs is None else {"in_specs": in_specs}
    return pl.pallas_call(
        body,
        out_shape=out_shape,
        **specs,
        out_specs=jax.tree.map(lambda _: IN_VMEM, out_shape),
        scratch_shapes=scratch,
        compiler_params=pltpu.CompilerParams(vmem_limit_bytes=VMEM),
        cost_estimate=pl.CostEstimate(
            flops=flops, bytes_accessed=sum(o.size * o.dtype.itemsize for o in outs), transcendentals=0
        ),
        name=name,
    )


def norm_features(x, first):
    values = x.astype(f32)
    norms = jnp.sum(values * values, axis=0, keepdims=True) * (-decay_rate)
    high = norms.astype(bf16).astype(f32)
    middle = (norms - high).astype(bf16).astype(f32)
    low = norms - high - middle
    at = lax.broadcasted_iota(jnp.int32, x.shape, 0)
    ones = 3 - first
    out = jnp.where((at >= ones) & (at < ones + 3), 1.0, 0.0)
    for k, piece in enumerate((high, middle, low)):
        out = jnp.where(at == first + k, piece, out)
    return out.astype(bf16)


def far_and_near():
    at = np.arange(math.prod(SIZES)).reshape(SIZES)
    far = at[..., 0].transpose(0, 3, 1, 4, 2).reshape(-1, 16)
    near = at[..., 1].transpose(1, 4, 2, 0, 3).reshape(far.shape)
    return np.concatenate([far, near]).tolist()


def product_kernel(place_ref, mine_ref, other_ref, out_ref, own_ref, row_side, col_side, dirs, parts):
    first = lax.rem(place_ref[0], 2) == 0
    me = lax.div(place_ref[0], 2)
    rhs = dirs.shape[0]
    dim = DEPTH // 2
    count_r = row_side.shape[1] // LANES
    count_c = col_side.shape[0] // LANES
    per_step = ROW_BLOCK // LANES

    def prepare_rows(k):
        x = jnp.where(first, other_ref[2 * k][0:dim], mine_ref[2 * k + 1][0:dim])
        here = slice(k * LANES, (k + 1) * LANES)
        row_side[0:dim, here] = (x.astype(f32) * (2.0 * decay_rate)).astype(bf16)
        row_side[dim:DEPTH, here] = norm_features(x, 0)

    def prepare_cols(k):
        both = jnp.where(first, mine_ref[k], other_ref[k])
        x = both[0:dim]
        here = slice(k * LANES, (k + 1) * LANES)
        col_side[here, :] = jnp.concatenate([x, norm_features(x, 3)], axis=0).T
        dirs[:, here] = both[dim : dim + rhs]

    def products(rows, cols):
        expo = jnp.dot(col_side[cols, :], row_side[:, rows], preferred_element_type=f32)
        kern = jnp.minimum((amplitude * jnp.exp2(expo * LOG2E)).astype(bf16), jnp.asarray(amplitude, bf16))
        return jnp.dot(dirs[:, cols], kern, preferred_element_type=f32)

    def store(i, total):
        for k in range(per_step):
            part = total[:, k * LANES : (k + 1) * LANES]
            out_ref[i * per_step + k] = part.astype(bf16)
            parts[i * per_step + k] = part

    chunk = count_c // COL_CHUNKS
    later = list(range(per_step, count_r))
    share = -(-len(later) // COL_CHUNKS)
    for k in range(per_step):
        prepare_rows(k)
    for k in range(chunk):
        prepare_cols(k)
    total = jnp.zeros((rhs, ROW_BLOCK), f32)
    for q in range(COL_CHUNKS):
        if q + 1 < COL_CHUNKS:
            for k in range((q + 1) * chunk, (q + 2) * chunk):
                prepare_cols(k)
        for k in later[q * share : (q + 1) * share]:
            prepare_rows(k)
        cols = slice(q * chunk * LANES, (q + 1) * chunk * LANES)
        total = total + products(slice(0, ROW_BLOCK), cols)
    store(0, total)

    def one_step(i, carry):
        here = pl.ds(pl.multiple_of(i * ROW_BLOCK, ROW_BLOCK), ROW_BLOCK)
        store(i, products(here, slice(0, count_c * LANES)))
        return carry

    lax.fori_loop(1, count_r // per_step, one_step, 0)
    own_ref[...] = parts[me]
    out_ref[me] = jnp.zeros((rhs, LANES), bf16)


def to_lanes(first, second):
    shape = (first.shape[0], LANES)
    at = lax.broadcasted_iota(jnp.int32, shape, 0)
    lane = lax.broadcasted_iota(jnp.int32, shape, 1)
    square = jnp.where(at == lane, first, jnp.where(at + LANES // 2 == lane, second, 0.0))
    return jnp.sum(square, axis=0, keepdims=True)


def sums_kernel(arrived_ref, own_ref, direction_ref, residual_ref, image_ref, sums_ref):
    direction = direction_ref[...]
    residual = residual_ref[...]
    image = noise_level * direction
    total = own_ref[...]
    for k in range(arrived_ref.shape[0]):
        total = total + arrived_ref[k].astype(f32)
    image = total + image
    image_ref[...] = image
    products = (residual * residual, direction * image, residual * image, image * image)
    rr_sum, pq_sum, rq_sum, qq_sum = (jnp.sum(v, axis=1, keepdims=True) for v in products)
    sums = jnp.concatenate([to_lanes(rr_sum, pq_sum), to_lanes(rq_sum, qq_sum)], axis=0)
    for k in range(sums_ref.shape[0]):
        sums_ref[k] = sums


def middle_kernel(arrived_ref, sums_ref):
    sums = jnp.sum(arrived_ref[...], axis=0)
    for k in range(sums_ref.shape[0]):
        sums_ref[k] = sums


def to_rows(row, rhs):
    square = jnp.broadcast_to(row, (rhs, LANES))
    at = lax.broadcasted_iota(jnp.int32, square.shape, 0)
    lane = lax.broadcasted_iota(jnp.int32, square.shape, 1)
    return (
        jnp.sum(jnp.where(at == lane, square, 0.0), axis=1, keepdims=True),
        jnp.sum(jnp.where(at + LANES // 2 == lane, square, 0.0), axis=1, keepdims=True),
    )


def last_kernel(arrived_ref, image_ref, solution_ref, residual_ref, direction_ref, s_ref, r_ref, d_ref):
    rhs = image_ref.shape[0]
    sums = jnp.sum(arrived_ref[...], axis=0)
    rr_sum, pq_sum = to_rows(sums[0:1], rhs)
    rq_sum, qq_sum = to_rows(sums[1:2], rhs)
    alpha = rr_sum / pq_sum
    beta = (rr_sum - 2.0 * alpha * rq_sum + alpha * alpha * qq_sum) / rr_sum
    direction = direction_ref[...]
    residual_next = residual_ref[...] - alpha * image_ref[...]
    s_ref[...] = solution_ref[...] + alpha * direction
    r_ref[...] = residual_next
    d_ref[...] = residual_next + beta * direction


def local(points, solution_field, residual, direction):
    dim, width = points.shape
    rhs = direction.shape[0]
    shape = jax.ShapeDtypeStruct
    both = jnp.concatenate([points, direction.astype(bf16)], axis=0)
    groups = far_and_near()
    peers = len(groups[0])
    both = lax.all_gather(jnp.pad(both, ((0, -both.shape[0] % 8), (0, 0))), "c", axis=0, tiled=True)
    both = both.reshape(2, -1, both.shape[1])
    mine = jnp.broadcast_to(both[None], (peers, *both.shape)).reshape(-1, *both.shape[1:])
    mine = lax.all_to_all(mine, ALL, 0, 0, axis_index_groups=groups, tiled=True)
    other = lax.ppermute(mine, "c", [(0, 1), (1, 0)])
    depth = 2 * peers * width
    pairs = depth * peers * width
    place = (2 * lax.axis_index(ROWS) + lax.axis_index("c")).reshape(1)
    partial, own = kernel_call(
        product_kernel,
        (shape((peers, rhs, width), bf16), shape((rhs, width), f32)),
        "products",
        flops=2 * pairs * (DEPTH + rhs),
        scratch=[
            pltpu.VMEM((DEPTH, peers * width), bf16),
            pltpu.VMEM((depth, DEPTH), bf16),
            pltpu.VMEM((rhs, depth), bf16),
            pltpu.VMEM((peers, rhs, width), f32),
        ],
        in_specs=[pl.BlockSpec(memory_space=pltpu.SMEM), IN_VMEM, IN_VMEM],
    )(place, mine, other)
    arrived = lax.all_to_all(partial, ROWS, 0, 0, tiled=True)
    image, sums = kernel_call(
        sums_kernel,
        (shape((rhs, width), f32), shape((lax.axis_size(SUM_1), 2, LANES), f32)),
        "sums",
    )(arrived, own, direction, residual)
    sums = lax.all_to_all(sums, SUM_1, 0, 0, tiled=True)
    sums = kernel_call(middle_kernel, shape((lax.axis_size(SUM_2), 2, LANES), f32), "middle")(sums)
    sums = lax.all_to_all(sums, SUM_2, 0, 0, tiled=True)
    out = shape((rhs, width), f32)
    return kernel_call(last_kernel, (out, out, out), "last")(
        sums, image, solution_field, residual, direction
    )


def solution(mesh):
    split = Mesh(mesh.devices.reshape(SIZES), ALL)
    spec = P(None, ALL)
    return jax.shard_map(
        local, mesh=split, in_specs=(spec,) * 4, out_specs=(spec,) * 3, check_vma=False
    )
```

```python
import functools
import math

import jax
import jax.numpy as jnp
import numpy as np
from jax import lax
from jax.experimental import pallas as pl
from jax.experimental.pallas import tpu as pltpu
from jax.sharding import Mesh
from jax.sharding import PartitionSpec as P

f32 = jnp.float32
bf16 = jnp.bfloat16

ALL = ("y", "zh", "xh", "xl", "zl", "c")
SIZES = (8, 4, 2, 2, 2, 2)
ROWS = ('zh', 'zl', 'xl')
SUM_1 = ("zh", "zl", "c")
SUM_2 = ("y", "xh", "xl")

amplitude = 1.0
decay_rate = 1.0 / 16.0
noise_level = 0.5
LOG2E = math.log2(math.e)
DEPTH = 128
LANES = 128
ROW_BLOCK = 1024
COL_CHUNKS = 4
VMEM = 50 * 2**20
IN_VMEM = pl.BlockSpec(memory_space=pltpu.VMEM)


def kernel_call(body, out_shape, name, flops=10**6, scratch=(), in_specs=None):
    outs = jax.tree.leaves(out_shape)
    specs = {} if in_specs is None else {"in_specs": in_specs}
    return pl.pallas_call(
        body,
        out_shape=out_shape,
        **specs,
        out_specs=jax.tree.map(lambda _: IN_VMEM, out_shape),
        scratch_shapes=scratch,
        compiler_params=pltpu.CompilerParams(vmem_limit_bytes=VMEM),
        cost_estimate=pl.CostEstimate(
            flops=flops, bytes_accessed=sum(o.size * o.dtype.itemsize for o in outs), transcendentals=0
        ),
        name=name,
    )


def norm_features(x, first):
    values = x.astype(f32)
    norms = jnp.sum(values * values, axis=0, keepdims=True) * (-decay_rate)
    high = norms.astype(bf16).astype(f32)
    middle = (norms - high).astype(bf16).astype(f32)
    low = norms - high - middle
    at = lax.broadcasted_iota(jnp.int32, x.shape, 0)
    ones = 3 - first
    out = jnp.where((at >= ones) & (at < ones + 3), 1.0, 0.0)
    for k, piece in enumerate((high, middle, low)):
        out = jnp.where(at == first + k, piece, out)
    return out.astype(bf16)


def far_and_near():
    at = np.arange(math.prod(SIZES)).reshape(SIZES)
    far = at[..., 0].transpose(1, 4, 3, 0, 2).reshape(-1, 16)
    near = at[..., 1].transpose(0, 2, 1, 4, 3).reshape(far.shape)
    return np.concatenate([far, near]).tolist()


def product_kernel(place_ref, mine_ref, other_ref, out_ref, own_ref, row_side, col_side, dirs, parts):
    first = lax.rem(place_ref[0], 2) == 0
    me = lax.div(place_ref[0], 2)
    rhs = dirs.shape[0]
    dim = DEPTH // 2
    count_r = row_side.shape[1] // LANES
    count_c = col_side.shape[0] // LANES
    per_step = ROW_BLOCK // LANES

    def prepare_rows(k):
        x = jnp.where(first, other_ref[2 * k][0:dim], mine_ref[2 * k + 1][0:dim])
        here = slice(k * LANES, (k + 1) * LANES)
        row_side[0:dim, here] = (x.astype(f32) * (2.0 * decay_rate)).astype(bf16)
        row_side[dim:DEPTH, here] = norm_features(x, 0)

    def prepare_cols(k):
        both = jnp.where(first, mine_ref[k], other_ref[k])
        x = both[0:dim]
        here = slice(k * LANES, (k + 1) * LANES)
        col_side[here, :] = jnp.concatenate([x, norm_features(x, 3)], axis=0).T
        dirs[:, here] = both[dim : dim + rhs]

    def products(rows, cols):
        expo = jnp.dot(col_side[cols, :], row_side[:, rows], preferred_element_type=f32)
        kern = jnp.minimum((amplitude * jnp.exp2(expo * LOG2E)).astype(bf16), jnp.asarray(amplitude, bf16))
        return jnp.dot(dirs[:, cols], kern, preferred_element_type=f32)

    def store(i, total):
        for k in range(per_step):
            part = total[:, k * LANES : (k + 1) * LANES]
            out_ref[i * per_step + k] = part.astype(bf16)
            parts[i * per_step + k] = part

    chunk = count_c // COL_CHUNKS
    later = list(range(per_step, count_r))
    share = -(-len(later) // COL_CHUNKS)
    for k in range(per_step):
        prepare_rows(k)
    for k in range(chunk):
        prepare_cols(k)
    total = jnp.zeros((rhs, ROW_BLOCK), f32)
    for q in range(COL_CHUNKS):
        if q + 1 < COL_CHUNKS:
            for k in range((q + 1) * chunk, (q + 2) * chunk):
                prepare_cols(k)
        for k in later[q * share : (q + 1) * share]:
            prepare_rows(k)
        cols = slice(q * chunk * LANES, (q + 1) * chunk * LANES)
        total = total + products(slice(0, ROW_BLOCK), cols)
    store(0, total)

    def one_step(i, carry):
        here = pl.ds(pl.multiple_of(i * ROW_BLOCK, ROW_BLOCK), ROW_BLOCK)
        store(i, products(here, slice(0, count_c * LANES)))
        return carry

    lax.fori_loop(1, count_r // per_step, one_step, 0)
    own_ref[...] = parts[me]
    out_ref[me] = jnp.zeros((rhs, LANES), bf16)


def to_lanes(first, second):
    shape = (first.shape[0], LANES)
    at = lax.broadcasted_iota(jnp.int32, shape, 0)
    lane = lax.broadcasted_iota(jnp.int32, shape, 1)
    square = jnp.where(at == lane, first, jnp.where(at + LANES // 2 == lane, second, 0.0))
    return jnp.sum(square, axis=0, keepdims=True)


def sums_kernel(arrived_ref, own_ref, direction_ref, residual_ref, image_ref, sums_ref):
    direction = direction_ref[...]
    residual = residual_ref[...]
    image = noise_level * direction
    total = own_ref[...]
    for k in range(arrived_ref.shape[0]):
        total = total + arrived_ref[k].astype(f32)
    image = total + image
    image_ref[...] = image
    products = (residual * residual, direction * image, residual * image, image * image)
    rr_sum, pq_sum, rq_sum, qq_sum = (jnp.sum(v, axis=1, keepdims=True) for v in products)
    sums = jnp.concatenate([to_lanes(rr_sum, pq_sum), to_lanes(rq_sum, qq_sum)], axis=0)
    for k in range(sums_ref.shape[0]):
        sums_ref[k] = sums


def middle_kernel(arrived_ref, sums_ref):
    sums = jnp.sum(arrived_ref[...], axis=0)
    for k in range(sums_ref.shape[0]):
        sums_ref[k] = sums


def to_rows(row, rhs):
    square = jnp.broadcast_to(row, (rhs, LANES))
    at = lax.broadcasted_iota(jnp.int32, square.shape, 0)
    lane = lax.broadcasted_iota(jnp.int32, square.shape, 1)
    return (
        jnp.sum(jnp.where(at == lane, square, 0.0), axis=1, keepdims=True),
        jnp.sum(jnp.where(at + LANES // 2 == lane, square, 0.0), axis=1, keepdims=True),
    )


def last_kernel(arrived_ref, image_ref, solution_ref, residual_ref, direction_ref, s_ref, r_ref, d_ref):
    rhs = image_ref.shape[0]
    sums = jnp.sum(arrived_ref[...], axis=0)
    rr_sum, pq_sum = to_rows(sums[0:1], rhs)
    rq_sum, qq_sum = to_rows(sums[1:2], rhs)
    alpha = rr_sum / pq_sum
    beta = (rr_sum - 2.0 * alpha * rq_sum + alpha * alpha * qq_sum) / rr_sum
    direction = direction_ref[...]
    residual_next = residual_ref[...] - alpha * image_ref[...]
    s_ref[...] = solution_ref[...] + alpha * direction
    r_ref[...] = residual_next
    d_ref[...] = residual_next + beta * direction


def local(points, solution_field, residual, direction):
    dim, width = points.shape
    rhs = direction.shape[0]
    shape = jax.ShapeDtypeStruct
    both = jnp.concatenate([points, direction.astype(bf16)], axis=0)
    groups = far_and_near()
    peers = len(groups[0])
    both = lax.all_gather(jnp.pad(both, ((0, -both.shape[0] % 8), (0, 0))), "c", axis=0, tiled=True)
    both = both.reshape(2, -1, both.shape[1])
    mine = jnp.broadcast_to(both[None], (peers, *both.shape)).reshape(-1, *both.shape[1:])
    mine = lax.all_to_all(mine, ALL, 0, 0, axis_index_groups=groups, tiled=True)
    other = lax.ppermute(mine, "c", [(0, 1), (1, 0)])
    depth = 2 * peers * width
    pairs = depth * peers * width
    place = (2 * lax.axis_index(ROWS) + lax.axis_index("c")).reshape(1)
    partial, own = kernel_call(
        product_kernel,
        (shape((peers, rhs, width), bf16), shape((rhs, width), f32)),
        "products",
        flops=2 * pairs * (DEPTH + rhs),
        scratch=[
            pltpu.VMEM((DEPTH, peers * width), bf16),
            pltpu.VMEM((depth, DEPTH), bf16),
            pltpu.VMEM((rhs, depth), bf16),
            pltpu.VMEM((peers, rhs, width), f32),
        ],
        in_specs=[pl.BlockSpec(memory_space=pltpu.SMEM), IN_VMEM, IN_VMEM],
    )(place, mine, other)
    arrived = lax.all_to_all(partial, ROWS, 0, 0, tiled=True)
    image, sums = kernel_call(
        sums_kernel,
        (shape((rhs, width), f32), shape((lax.axis_size(SUM_1), 2, LANES), f32)),
        "sums",
    )(arrived, own, direction, residual)
    sums = lax.all_to_all(sums, SUM_1, 0, 0, tiled=True)
    sums = kernel_call(middle_kernel, shape((lax.axis_size(SUM_2), 2, LANES), f32), "middle")(sums)
    sums = lax.all_to_all(sums, SUM_2, 0, 0, tiled=True)
    out = shape((rhs, width), f32)
    return kernel_call(last_kernel, (out, out, out), "last")(
        sums, image, solution_field, residual, direction
    )


def solution(mesh):
    split = Mesh(mesh.devices.reshape(SIZES), ALL)
    spec = P(None, ALL)
    return jax.shard_map(
        local, mesh=split, in_specs=(spec,) * 4, out_specs=(spec,) * 3, check_vma=False
    )
```

```python
import functools
import math

import jax
import jax.numpy as jnp
import numpy as np
from jax import lax
from jax.experimental import pallas as pl
from jax.experimental.pallas import tpu as pltpu
from jax.sharding import Mesh
from jax.sharding import PartitionSpec as P

f32 = jnp.float32
bf16 = jnp.bfloat16

ALL = ("y", "zh", "xh", "xl", "zl", "c")
SIZES = (8, 4, 2, 2, 2, 2)
ROWS = ('y', 'xl')
SUM_1 = ("zh", "zl", "c")
SUM_2 = ("y", "xh", "xl")

amplitude = 1.0
decay_rate = 1.0 / 16.0
noise_level = 0.5
LOG2E = math.log2(math.e)
DEPTH = 128
LANES = 128
ROW_BLOCK = 1024
COL_CHUNKS = 4
VMEM = 50 * 2**20
IN_VMEM = pl.BlockSpec(memory_space=pltpu.VMEM)


def kernel_call(body, out_shape, name, flops=10**6, scratch=(), in_specs=None):
    outs = jax.tree.leaves(out_shape)
    specs = {} if in_specs is None else {"in_specs": in_specs}
    return pl.pallas_call(
        body,
        out_shape=out_shape,
        **specs,
        out_specs=jax.tree.map(lambda _: IN_VMEM, out_shape),
        scratch_shapes=scratch,
        compiler_params=pltpu.CompilerParams(vmem_limit_bytes=VMEM),
        cost_estimate=pl.CostEstimate(
            flops=flops, bytes_accessed=sum(o.size * o.dtype.itemsize for o in outs), transcendentals=0
        ),
        name=name,
    )


def norm_features(x, first):
    values = x.astype(f32)
    norms = jnp.sum(values * values, axis=0, keepdims=True) * (-decay_rate)
    high = norms.astype(bf16).astype(f32)
    middle = (norms - high).astype(bf16).astype(f32)
    low = norms - high - middle
    at = lax.broadcasted_iota(jnp.int32, x.shape, 0)
    ones = 3 - first
    out = jnp.where((at >= ones) & (at < ones + 3), 1.0, 0.0)
    for k, piece in enumerate((high, middle, low)):
        out = jnp.where(at == first + k, piece, out)
    return out.astype(bf16)


def far_and_near():
    at = np.arange(math.prod(SIZES)).reshape(SIZES)
    far = at[..., 1].transpose(0, 3, 1, 4, 2).reshape(-1, 16)
    near = at[..., 0].transpose(1, 4, 2, 0, 3).reshape(far.shape)
    return np.concatenate([far, near]).tolist()


def product_kernel(place_ref, mine_ref, other_ref, out_ref, own_ref, row_side, col_side, dirs, parts):
    first = lax.rem(place_ref[0], 2) == 1
    me = lax.div(place_ref[0], 2)
    rhs = dirs.shape[0]
    dim = DEPTH // 2
    count_r = row_side.shape[1] // LANES
    count_c = col_side.shape[0] // LANES
    per_step = ROW_BLOCK // LANES

    def prepare_rows(k):
        x = jnp.where(first, other_ref[2 * k + 1][0:dim], mine_ref[2 * k][0:dim])
        here = slice(k * LANES, (k + 1) * LANES)
        row_side[0:dim, here] = (x.astype(f32) * (2.0 * decay_rate)).astype(bf16)
        row_side[dim:DEPTH, here] = norm_features(x, 0)

    def prepare_cols(k):
        both = jnp.where(first, mine_ref[k], other_ref[k])
        x = both[0:dim]
        here = slice(k * LANES, (k + 1) * LANES)
        col_side[here, :] = jnp.concatenate([x, norm_features(x, 3)], axis=0).T
        dirs[:, here] = both[dim : dim + rhs]

    def products(rows, cols):
        expo = jnp.dot(col_side[cols, :], row_side[:, rows], preferred_element_type=f32)
        kern = jnp.minimum((amplitude * jnp.exp2(expo * LOG2E)).astype(bf16), jnp.asarray(amplitude, bf16))
        return jnp.dot(dirs[:, cols], kern, preferred_element_type=f32)

    def store(i, total):
        for k in range(per_step):
            part = total[:, k * LANES : (k + 1) * LANES]
            out_ref[i * per_step + k] = part.astype(bf16)
            parts[i * per_step + k] = part

    chunk = count_c // COL_CHUNKS
    later = list(range(per_step, count_r))
    share = -(-len(later) // COL_CHUNKS)
    for k in range(per_step):
        prepare_rows(k)
    for k in range(chunk):
        prepare_cols(k)
    total = jnp.zeros((rhs, ROW_BLOCK), f32)
    for q in range(COL_CHUNKS):
        if q + 1 < COL_CHUNKS:
            for k in range((q + 1) * chunk, (q + 2) * chunk):
                prepare_cols(k)
        for k in later[q * share : (q + 1) * share]:
            prepare_rows(k)
        cols = slice(q * chunk * LANES, (q + 1) * chunk * LANES)
        total = total + products(slice(0, ROW_BLOCK), cols)
    store(0, total)

    def one_step(i, carry):
        here = pl.ds(pl.multiple_of(i * ROW_BLOCK, ROW_BLOCK), ROW_BLOCK)
        store(i, products(here, slice(0, count_c * LANES)))
        return carry

    lax.fori_loop(1, count_r // per_step, one_step, 0)
    own_ref[...] = parts[me]
    out_ref[me] = jnp.zeros((rhs, LANES), bf16)


def to_lanes(first, second):
    shape = (first.shape[0], LANES)
    at = lax.broadcasted_iota(jnp.int32, shape, 0)
    lane = lax.broadcasted_iota(jnp.int32, shape, 1)
    square = jnp.where(at == lane, first, jnp.where(at + LANES // 2 == lane, second, 0.0))
    return jnp.sum(square, axis=0, keepdims=True)


def sums_kernel(arrived_ref, own_ref, direction_ref, residual_ref, image_ref, sums_ref):
    direction = direction_ref[...]
    residual = residual_ref[...]
    image = noise_level * direction
    total = own_ref[...]
    for k in range(arrived_ref.shape[0]):
        total = total + arrived_ref[k].astype(f32)
    image = total + image
    image_ref[...] = image
    products = (residual * residual, direction * image, residual * image, image * image)
    rr_sum, pq_sum, rq_sum, qq_sum = (jnp.sum(v, axis=1, keepdims=True) for v in products)
    sums = jnp.concatenate([to_lanes(rr_sum, pq_sum), to_lanes(rq_sum, qq_sum)], axis=0)
    for k in range(sums_ref.shape[0]):
        sums_ref[k] = sums


def middle_kernel(arrived_ref, sums_ref):
    sums = jnp.sum(arrived_ref[...], axis=0)
    for k in range(sums_ref.shape[0]):
        sums_ref[k] = sums


def to_rows(row, rhs):
    square = jnp.broadcast_to(row, (rhs, LANES))
    at = lax.broadcasted_iota(jnp.int32, square.shape, 0)
    lane = lax.broadcasted_iota(jnp.int32, square.shape, 1)
    return (
        jnp.sum(jnp.where(at == lane, square, 0.0), axis=1, keepdims=True),
        jnp.sum(jnp.where(at + LANES // 2 == lane, square, 0.0), axis=1, keepdims=True),
    )


def last_kernel(arrived_ref, image_ref, solution_ref, residual_ref, direction_ref, s_ref, r_ref, d_ref):
    rhs = image_ref.shape[0]
    sums = jnp.sum(arrived_ref[...], axis=0)
    rr_sum, pq_sum = to_rows(sums[0:1], rhs)
    rq_sum, qq_sum = to_rows(sums[1:2], rhs)
    alpha = rr_sum / pq_sum
    beta = (rr_sum - 2.0 * alpha * rq_sum + alpha * alpha * qq_sum) / rr_sum
    direction = direction_ref[...]
    residual_next = residual_ref[...] - alpha * image_ref[...]
    s_ref[...] = solution_ref[...] + alpha * direction
    r_ref[...] = residual_next
    d_ref[...] = residual_next + beta * direction


def local(points, solution_field, residual, direction):
    dim, width = points.shape
    rhs = direction.shape[0]
    shape = jax.ShapeDtypeStruct
    both = jnp.concatenate([points, direction.astype(bf16)], axis=0)
    groups = far_and_near()
    peers = len(groups[0])
    both = lax.all_gather(jnp.pad(both, ((0, -both.shape[0] % 8), (0, 0))), "c", axis=0, tiled=True)
    both = both.reshape(2, -1, both.shape[1])
    mine = jnp.broadcast_to(both[None], (peers, *both.shape)).reshape(-1, *both.shape[1:])
    mine = lax.all_to_all(mine, ALL, 0, 0, axis_index_groups=groups, tiled=True)
    other = lax.ppermute(mine, "c", [(0, 1), (1, 0)])
    depth = 2 * peers * width
    pairs = depth * peers * width
    place = (2 * lax.axis_index(ROWS) + lax.axis_index("c")).reshape(1)
    partial, own = kernel_call(
        product_kernel,
        (shape((peers, rhs, width), bf16), shape((rhs, width), f32)),
        "products",
        flops=2 * pairs * (DEPTH + rhs),
        scratch=[
            pltpu.VMEM((DEPTH, peers * width), bf16),
            pltpu.VMEM((depth, DEPTH), bf16),
            pltpu.VMEM((rhs, depth), bf16),
            pltpu.VMEM((peers, rhs, width), f32),
        ],
        in_specs=[pl.BlockSpec(memory_space=pltpu.SMEM), IN_VMEM, IN_VMEM],
    )(place, mine, other)
    arrived = lax.all_to_all(partial, ROWS, 0, 0, tiled=True)
    image, sums = kernel_call(
        sums_kernel,
        (shape((rhs, width), f32), shape((lax.axis_size(SUM_1), 2, LANES), f32)),
        "sums",
    )(arrived, own, direction, residual)
    sums = lax.all_to_all(sums, SUM_1, 0, 0, tiled=True)
    sums = kernel_call(middle_kernel, shape((lax.axis_size(SUM_2), 2, LANES), f32), "middle")(sums)
    sums = lax.all_to_all(sums, SUM_2, 0, 0, tiled=True)
    out = shape((rhs, width), f32)
    return kernel_call(last_kernel, (out, out, out), "last")(
        sums, image, solution_field, residual, direction
    )


def solution(mesh):
    split = Mesh(mesh.devices.reshape(SIZES), ALL)
    spec = P(None, ALL)
    return jax.shard_map(
        local, mesh=split, in_specs=(spec,) * 4, out_specs=(spec,) * 3, check_vma=False
    )
```
